32 devices in a mesh: groups: 2 (over x), ctx: 16 (over z, y, core).
Axes of the slice: x: 2, y: 2, z: 4, core: 2. Of those that a mesh axis runs over, the one named last changes fastest.
Arguments:
- events: bfloat16 [16384, 1024], P(('groups', 'ctx')), parts along dimension 0, may hold values from -6 to 6
- w_in: bfloat16 [1024, 4096], replicated, may hold values from -0.1875 to 0.1875
- w_out: bfloat16 [1024, 1024], replicated, may hold values from -0.1875 to 0.1875
- rel_bias: float32 [16, 16], replicated, may hold values from -3 to 3
- lengths: int32 [8], P('groups'), parts along dimension 0, may hold values from 1 to 4096, as said below
- block_lists: int32 [32, 2], P(('groups', 'ctx')), parts along dimension 0, may hold values from 1 to 4, as said below
- candidates: int32 [32, 128], P('groups'), parts along dimension 0, may hold values from 0 to 8191, as said below
Outputs:
- layer_output: bfloat16 [16384, 1024], P(('groups', 'ctx')), parts along dimension 0
- next_score: float32 [16384], P(('groups', 'ctx')), parts along dimension 0
- candidate_score_table: float32 [16384, 128], P(('groups', 'ctx')), parts along dimension 0
The draws below stay inside these ranges and needn't reach their ends.
There are 2 independent parts, one for each index of `groups`. The reference program is written for one: setup_inputs(seed, part) draws one part's arguments, and reference() takes and returns one part's arrays. A program takes and returns all parts, laid end to end along the dimension named above; an argument that names none is the same for every part. Nothing has to cross between parts.
Inputs may be any that keep to these rules, and one draw needn't show every extreme that they name: `lengths`: the first user has exactly 4096 events. `block_lists`: each row holds 2 different distances; row 0 lists distance 1. `candidates`: of one row's 128 rows at most 16 lie in one block, and exactly 16 in some block.
All inputs are finite; a program needn't handle non-finite values.
Results may differ from the reference program's by a relative error of at most 0.007.
Values may be sent and summed in bfloat16 or wider, within the bound.
A program may use at most 128 MiB of HBM per device.

```python
import jax
import jax.numpy as jnp
from jax import lax

HEADS = 16
D = 1024
ROWS = 512
SPAN = 4
NSEL = 2
NB = 16
NCAND = 128
TOKENS = 8192
USERS = 4
MOSTLEN = 4096


def draw_lengths(key, part):
    rest_total = TOKENS - MOSTLEN
    cut_count = USERS - 2
    cuts = jnp.sort(jax.random.permutation(key, rest_total - 1)[:cut_count] + 1).astype(jnp.int32)
    bounds = jnp.concatenate([jnp.zeros((1,), jnp.int32), cuts, jnp.full((1,), rest_total, jnp.int32)])
    others = bounds[1:] - bounds[:-1]
    return jnp.concatenate([jnp.full((1,), MOSTLEN, jnp.int32), others]).astype(jnp.int32)


def draw_block_lists(key, part):
    total_block_count = TOKENS // ROWS
    row_keys = jax.random.split(key, total_block_count + 1)
    chosen = jax.random.randint(row_keys[total_block_count], (), 1, total_block_count)

    def one_row(row_key, row_num):
        shuffled = jax.random.permutation(row_key, SPAN)
        start_at = jnp.argmax((shuffled == SPAN - 1).astype(jnp.int32))
        turned = jnp.roll(shuffled, -start_at)
        shuffled_first = jnp.where(row_num == chosen, turned, shuffled)
        zero_at = jnp.argmax((shuffled == 0).astype(jnp.int32))
        zero_first = jnp.roll(shuffled, -zero_at)
        shuffled_first = jnp.where(row_num == 0, zero_first, shuffled_first)
        return shuffled_first[:NSEL] + 1
    return jax.vmap(one_row)(row_keys[:total_block_count], jnp.arange(total_block_count)).astype(jnp.int32)


def draw_candidates(key, part):
    total_block_count = TOKENS // ROWS
    slot_cap = 2 * NCAND // total_block_count
    row_keys = jax.random.split(key, total_block_count)

    def one_row(row_key):
        split_keys = jax.random.split(row_key, 4)
        full_owner = jax.random.randint(split_keys[0], (), 0, total_block_count)
        slot_list = jax.random.permutation(split_keys[1], (total_block_count - 1) * slot_cap)[:NCAND - slot_cap]
        other_owner = slot_list // slot_cap
        other_owner = other_owner + (other_owner >= full_owner).astype(jnp.int32)
        owners = jnp.concatenate([jnp.full((slot_cap,), full_owner, jnp.int32), other_owner.astype(jnp.int32)])
        owners = jax.random.permutation(split_keys[2], owners)
        local_row = jax.random.randint(split_keys[3], (NCAND,), 0, ROWS)
        return owners * ROWS + local_row
    return jax.vmap(one_row)(row_keys).astype(jnp.int32)


def level_of(own_key, shape, shards, least, largest):
    def one(position, shards_of):
        heights = jax.random.uniform(jax.random.fold_in(jax.random.fold_in(own_key, 6), position), (shards_of,), jnp.float32, least / len(shards), largest / len(shards))
        return jnp.repeat(jnp.exp(heights), shape[position] // shards_of).reshape((-1,) + (1,) * (len(shape) - position - 1))

    loudness = one(*shards[0])
    for cut in shards[1:]:
        loudness = loudness * one(*cut)
    return loudness


def bell_draw(rng, extent, scale, reach, pieces=(), kind=jnp.bfloat16):
    gain = level_of(rng, extent, pieces, -0.22, 0.18) if pieces else 1.0
    entries = jax.random.normal(rng, extent, jnp.float32) * scale * gain
    return jnp.minimum(jnp.maximum(entries, -reach), reach).astype(kind)


def setup_inputs(seed: int = 0, part: int = 0) -> dict:
    key_list = jax.random.split(jax.random.key(seed), 8)
    part_keys = jax.random.split(jax.random.fold_in(key_list[7], part), 8)
    events = bell_draw(part_keys[0], (TOKENS, D), 1.0, 6.0, ((0, 16),))
    w_in = bell_draw(key_list[1], (D, 4 * D), D ** -0.5, 0.1875)
    w_out = bell_draw(key_list[2], (D, D), D ** -0.5, 0.1875)
    rel_bias = bell_draw(key_list[3], (HEADS, NB), 1.0, 3.0, (), jnp.float32)
    lengths = draw_lengths(jax.random.fold_in(jax.random.fold_in(key_list[7], part), 71), part)
    block_lists = draw_block_lists(jax.random.fold_in(jax.random.fold_in(key_list[7], part), 71), part)
    candidates = draw_candidates(jax.random.fold_in(jax.random.fold_in(key_list[7], part), 71), part)
    return dict(events=events, w_in=w_in, w_out=w_out, rel_bias=rel_bias, lengths=lengths, block_lists=block_lists, candidates=candidates)


def layer_norm(values):
    values = values.astype(jnp.float32)
    center = values - lax.optimization_barrier(jnp.mean(values, -1, keepdims=True))
    spread = lax.optimization_barrier(jnp.mean(center * center, -1, keepdims=True))
    return center * lax.rsqrt(spread + 1e-05)

def bucket_bias(distance, rel_bias):
    buckets = rel_bias.shape[1]
    bucket = jnp.zeros(distance.shape, jnp.int32)
    for degree in range(buckets - 1):
        bucket = bucket + (distance >= 2 ** degree).astype(jnp.int32)
    rel_terms = jnp.zeros((rel_bias.shape[0],) + distance.shape, rel_bias.dtype)
    for degree in range(buckets):
        rel_terms = jnp.where((bucket == degree)[None], rel_bias[:, degree][:, None, None], rel_terms)
    return rel_terms

def user_of(positions, user_ends):
    return lax.optimization_barrier(jnp.sum((positions[:, None] >= user_ends[None, :]).astype(jnp.int32), axis=1))

def attend(queries, query_pos, query_user, key_rows, value_rows, key_pos, key_user, rel_bias):
    attention_scale = queries.shape[-1] ** (-0.5)
    scores = jnp.einsum('qhd,khd->hqk', queries.astype(jnp.float32), key_rows.astype(jnp.float32))
    distance = query_pos[:, None] - key_pos[None, :]
    rel_terms = bucket_bias(distance, rel_bias)
    allowed = (distance >= 0) & (query_user[:, None] == key_user[None, :])
    weights = jnp.where(allowed[None], jax.nn.silu(scores * attention_scale + rel_terms), 0.0).astype(jnp.bfloat16)
    return jnp.einsum('hqk,khd->qhd', weights.astype(jnp.float32), value_rows.astype(jnp.float32))

def reference(events, w_in, w_out, rel_bias, lengths, block_lists, candidates):
    total_rows, hidden_width = events.shape
    total_block_count, pick_count = block_lists.shape
    event_row_count = total_rows // total_block_count
    head_count = rel_bias.shape[0]
    head_size = hidden_width // head_count
    user_ends = jnp.cumsum(lengths).astype(jnp.int32)
    row_index = jnp.arange(total_rows, dtype=jnp.int32)
    positions = ((row_index + total_rows // 4) % total_rows).astype(jnp.int32)
    users = user_of(positions, user_ends)
    normed = layer_norm(events).astype(jnp.bfloat16)
    projected = jax.nn.silu(jnp.dot(normed, w_in, preferred_element_type=jnp.float32)).astype(jnp.bfloat16)
    gate_u = projected[:, :hidden_width]

    def shaped(columns):
        return columns.reshape(total_block_count, event_row_count, head_count, head_size)
    queries = shaped(projected[:, hidden_width:2 * hidden_width])
    value_rows = shaped(projected[:, 2 * hidden_width:3 * hidden_width])
    key_rows = shaped(projected[:, 3 * hidden_width:])
    block_pos = positions.reshape(total_block_count, event_row_count)
    block_users = users.reshape(total_block_count, event_row_count)

    def per_block(block_num):
        running = attend(queries[block_num], block_pos[block_num], block_users[block_num], key_rows[block_num], value_rows[block_num], block_pos[block_num], block_users[block_num], rel_bias)
        for pick_num in range(pick_count):
            source = ((block_num - block_lists[block_num, pick_num]) % total_block_count).astype(jnp.int32)
            running = running + attend(queries[block_num], block_pos[block_num], block_users[block_num], key_rows[source], value_rows[source], block_pos[source], block_users[source], rel_bias)
        return running
    attended = lax.map(per_block, jnp.arange(total_block_count, dtype=jnp.int32)).reshape(total_rows, hidden_width)
    gated_rows = (layer_norm(attended) * gate_u.astype(jnp.float32)).astype(jnp.bfloat16)
    layer_output = (events.astype(jnp.float32) + jnp.dot(gated_rows, w_out, preferred_element_type=jnp.float32)).astype(jnp.bfloat16)
    attention_scale = hidden_width ** (-0.5)
    following = jnp.concatenate([events[1:], events[:1]], axis=0)
    next_user = user_of(positions + 1, user_ends)
    inner = lax.optimization_barrier(jnp.sum(layer_output.astype(jnp.float32) * following.astype(jnp.float32), axis=1)) * attention_scale
    next_score = jnp.where(next_user == users, inner, 0.0)
    candidate_row_list = events[candidates]
    candidate_score_table = jnp.einsum('wza,wra->wzr', layer_output.reshape(total_block_count, event_row_count, hidden_width).astype(jnp.float32), candidate_row_list.astype(jnp.float32)) * attention_scale
    return (layer_output, next_score, candidate_score_table.reshape(total_rows, candidates.shape[1]))
```

```python
import jax
import jax.numpy as jnp
from jax import lax
from jax.experimental import pallas as pl
from jax.experimental.pallas import tpu as pltpu
from jax.sharding import PartitionSpec as P

SPAN = 4
NEG = -1e30
TILE = 128
PAIR = 128
VMEM_LIMIT = 56 * 1024 * 1024
BUFFER_OF = ((6, 5, 4, 3), (0, 5, 6, 3), (2, 1, 4, 3), (0, 1, 2, 3))
NBUF = 7

NT = (((1,), (1,)), ((), ()))


def user_of(positions, user_ends):
    return jnp.sum((positions[:, None] >= user_ends[None, :]).astype(jnp.int32), axis=1)


def half_silu(u):
    return u * jnp.tanh(u) + u


def normalize(x):
    center = x - jnp.mean(x, -1, keepdims=True)
    spread = jnp.mean(center * center, -1, keepdims=True)
    return center * lax.rsqrt(spread + 1e-05)


def bucket_of(distance, buckets):
    return min(int(distance).bit_length(), buckets - 1) if distance > 0 else 0


def bias_tile(rel_ref, head, step, buckets):
    if step < 0:
        return jnp.full((TILE, TILE), NEG, jnp.float32)
    row = lax.broadcasted_iota(jnp.int32, (TILE, TILE), 0)
    col = lax.broadcasted_iota(jnp.int32, (TILE, TILE), 1)
    diff = row - col
    first = bucket_of(step * TILE - TILE + 1, buckets)
    last = bucket_of(step * TILE + TILE - 1, buckets)
    value = jnp.full((TILE, TILE), rel_ref[head, first] * 0.5, jnp.float32)
    for b in range(first + 1, last + 1):
        value = jnp.where(diff >= 2 ** (b - 1) - step * TILE, rel_ref[head, b] * 0.5, value)
    if step == 0:
        value = jnp.where(diff >= 0, value, NEG)
    return value


def fill_slab(slab, index, rel_ref, head, top, width, buckets):
    for step in range(top - width + 1, top + 2):
        tile = bias_tile(rel_ref, head, step, buckets)
        for a in range(2):
            p = top + a - step
            if 0 <= p < width:
                slab[index, a * TILE : (a + 1) * TILE, p * TILE : (p + 1) * TILE] = tile


def pair_operands(q, k, v, qm, hot):
    low = lax.broadcasted_iota(jnp.int32, (1, PAIR), 1) < PAIR // 2
    zero = jnp.zeros((), jnp.bfloat16)
    for side in range(2):
        mine = low if side == 0 else jnp.logical_not(low)
        yield (
            jnp.where(mine, q, qm),
            jnp.where(mine, k, hot),
            jnp.where(mine, v, zero),
        )


def first_kernel(
    x_ref, w_hbm, rel_ref, qm_ref, hot_ref, gate_ref, q_ref, att_ref, w, normed, k_ref, v_ref, slab, sems
):
    rows, width = x_ref.shape
    heads, buckets = rel_ref.shape
    order = (1, 3, 2, 0)
    copies = {
        g: pltpu.make_async_copy(
            w_hbm.at[:, g * width : (g + 1) * width], w.at[g], sems.at[g]
        )
        for g in order
    }
    for g in order:
        copies[g].start()
    normed[...] = normalize(x_ref[...].astype(jnp.float32)).astype(jnp.bfloat16)

    def project(g, out, scale):
        def step(j, carry):
            cols = pl.ds(pl.multiple_of(j * 256, 256), 256)
            u = 0.5 * jnp.dot(normed[...], w[g, :, cols], preferred_element_type=jnp.float32)
            y = half_silu(u).astype(jnp.bfloat16)
            out[:, cols] = y if scale is None else y * jnp.asarray(scale, jnp.bfloat16)
            return carry

        copies[g].wait()
        lax.fori_loop(0, width // 256, step, 0)

    project(1, q_ref, 0.5 * (width // heads) ** -0.5)
    project(3, k_ref, None)
    project(2, v_ref, None)
    project(0, gate_ref, None)

    half = rows // 2

    def pair(hp, carry):
        cols = pl.ds(pl.multiple_of(hp * PAIR, PAIR), PAIR)
        for side in range(2):
            fill_slab(slab, side, rel_ref, 2 * hp + side, 2, 4, buckets)
        tops = []
        for side, (q, k, v) in enumerate(
            pair_operands(q_ref[:, cols], k_ref[:, cols], v_ref[:, cols], qm_ref[...], hot_ref[...])
        ):
            s0 = lax.dot_general(q[:half], k[:half], NT, preferred_element_type=jnp.float32)
            s1 = lax.dot_general(q[half:], k, NT, preferred_element_type=jnp.float32)
            w0 = half_silu(s0 + slab[side, :, half:]).astype(jnp.bfloat16)
            w1 = half_silu(s1 + slab[side]).astype(jnp.bfloat16)
            tops.append(
                (
                    jnp.dot(w0, v[:half], preferred_element_type=jnp.float32),
                    jnp.dot(w1, v, preferred_element_type=jnp.float32),
                )
            )
        att_ref[:half, cols] = tops[0][0] + tops[1][0]
        att_ref[half:, cols] = tops[0][1] + tops[1][1]
        return carry

    lax.fori_loop(0, heads // 2, pair, 0)


def second_kernel(
    info_ref, rel_ref, x_ref, gate_ref, q_ref, own_ref, qm_ref, hot_ref, cand_ref, follow_ref, ok_ref,
    w_hbm, wout_hbm, *rest
):
    bufs = rest[:NBUF]
    out_ref, next_ref, table_ref = rest[NBUF : NBUF + 3]
    picked, wkv, wout, normed, kv, att, slab, sems = rest[NBUF + 3 :]
    rows, width = x_ref.shape
    heads, buckets = rel_ref.shape
    picks = hot_ref.shape[0]
    half = rows // 2
    for p in range(picks):
        for n in range(NBUF):
            @pl.when(info_ref[p, 0] == n)
            def _():
                pltpu.make_async_copy(bufs[n], picked.at[p], sems.at[p]).start()
    w_copy = pltpu.make_async_copy(w_hbm.at[:, 2 * width :], wkv, sems.at[picks])
    o_copy = pltpu.make_async_copy(wout_hbm, wout, sems.at[picks + 1])
    w_copy.start()
    o_copy.start()
    att[...] = own_ref[...]
    for p in range(picks):
        pltpu.make_async_copy(bufs[0], picked.at[p], sems.at[p]).wait()
    w_copy.wait()
    for p in range(picks):
        @pl.when(info_ref[p, 2] == 1)
        def _(p=p):
            distance = info_ref[p, 1]
            normed[...] = normalize(picked[p].astype(jnp.float32)).astype(jnp.bfloat16)

            def step(j, carry):
                cols = pl.ds(pl.multiple_of(j * 256, 256), 256)
                u = 0.5 * jnp.dot(normed[...], wkv[:, cols], preferred_element_type=jnp.float32)
                kv[:, cols] = half_silu(u).astype(jnp.bfloat16)
                return carry

            lax.fori_loop(0, 2 * width // 256, step, 0)
            for d in range(1, SPAN + 1):
                @pl.when(distance == d)
                def _(d=d):
                    def fill(h, carry):
                        fill_slab(slab, h, rel_ref, h, (rows // TILE) * d + 2, 6, buckets)
                        return carry

                    lax.fori_loop(0, heads, fill, 0)

            def pair(hp, carry):
                cols = pl.ds(pl.multiple_of(hp * PAIR, PAIR), PAIR)
                kcols = pl.ds(pl.multiple_of(width + hp * PAIR, PAIR), PAIR)
                tops = []
                for side, (q, k, v) in enumerate(
                    pair_operands(q_ref[:, cols], kv[:, kcols], kv[:, cols], qm_ref[...], hot_ref[p])
                ):
                    h = 2 * hp + side
                    s0 = lax.dot_general(q[:half], k, NT, preferred_element_type=jnp.float32)
                    s1 = lax.dot_general(q[half:], k, NT, preferred_element_type=jnp.float32)
                    w0 = half_silu(s0 + slab[h, :, half:]).astype(jnp.bfloat16)
                    w1 = half_silu(s1 + slab[h, :, :rows]).astype(jnp.bfloat16)
                    tops.append(
                        (
                            jnp.dot(w0, v, preferred_element_type=jnp.float32),
                            jnp.dot(w1, v, preferred_element_type=jnp.float32),
                        )
                    )
                att[:half, cols] += tops[0][0] + tops[1][0]
                att[half:, cols] += tops[0][1] + tops[1][1]
                return carry

            lax.fori_loop(0, heads // 2, pair, 0)
    o_copy.wait()
    scale = width**-0.5

    def finish(r, carry):
        rs = pl.ds(pl.multiple_of(r * 256, 256), 256)
        gated = (normalize(att[rs, :]) * gate_ref[rs, :].astype(jnp.float32)).astype(jnp.bfloat16)
        added = jnp.dot(gated, wout[...], preferred_element_type=jnp.float32)
        layer = (x_ref[rs, :].astype(jnp.float32) + added).astype(jnp.bfloat16)
        out_ref[rs, :] = layer
        inner = jnp.sum(
            layer.astype(jnp.float32) * follow_ref[rs, :].astype(jnp.float32), axis=1, keepdims=True
        )
        next_ref[rs, :] = jnp.where(ok_ref[rs, :] > 0, inner * scale, 0.0)
        table_ref[rs, :] = (
            lax.dot_general(layer, cand_ref[...], NT, preferred_element_type=jnp.float32) * scale
        )
        return carry

    lax.fori_loop(0, rows // 256, finish, 0)


def slot_ids(request, ctx_size, event_row_count, slot_cap):
    owner_dev = request // event_row_count
    local_row = request % event_row_count
    owner_hits = (owner_dev[:, None] == jnp.arange(ctx_size, dtype=jnp.int32)[None, :]).astype(
        jnp.int32
    )
    slot_rank = jnp.sum(jnp.cumsum(owner_hits, axis=0) * owner_hits, axis=1) - 1
    slot_id = owner_dev * slot_cap + slot_rank
    slot_hits = slot_id[:, None] == jnp.arange(ctx_size * slot_cap, dtype=jnp.int32)[None, :]
    row_ids = jnp.sum(jnp.where(slot_hits, local_row[:, None] + 1, 0), axis=0) - 1
    return (row_ids.reshape(ctx_size, slot_cap), slot_hits)


def received(events, count):
    planes = count // SPAN
    shift = planes // 4

    def flows(plane):
        later = (plane + shift) % planes + 1
        return later < planes and later != planes // 2

    def inside(moves, wanted=None):
        return [
            (p * SPAN + s, p * SPAN + t)
            for p in range(planes)
            if wanted is None or wanted(p)
            for s, t in moves
        ]

    def fed(plane):
        return flows((plane - 1) % planes)

    across = [
        (p * SPAN + l, (p * SPAN + l + SPAN) % count)
        for p in range(planes)
        if flows(p)
        for l in range(SPAN)
    ]
    b1 = lax.ppermute(events, "ctx", across)
    a2 = lax.ppermute(events, "ctx", inside(((0, 2), (1, 3))))
    a1 = lax.ppermute(events, "ctx", inside(((0, 1), (2, 3))))
    b3 = lax.ppermute(b1, "ctx", inside(((2, 0), (3, 1)), fed))
    b2 = lax.ppermute(b1, "ctx", inside(((1, 0), (3, 2)), fed))
    a3 = lax.ppermute(a2, "ctx", inside(((2, 3), (3, 2))))
    b4 = lax.ppermute(b3, "ctx", inside(((0, 1), (1, 0)), fed))
    return (a1, a2, a3, b1, b2, b3, b4)


def fetch_candidates(events, candidates, ctx_size, my_index):
    event_row_count, hidden_width = events.shape
    cand_count = candidates.shape[1]
    slot_cap = 2 * cand_count // ctx_size
    own_request = lax.dynamic_slice_in_dim(candidates, my_index, 1, 0)[0]
    own_hits = slot_ids(own_request, ctx_size, event_row_count, slot_cap)[1]
    every_ids = jax.vmap(lambda request: slot_ids(request, ctx_size, event_row_count, slot_cap)[0])(
        candidates
    )
    my_part = lax.dynamic_index_in_dim(every_ids, my_index, 1, keepdims=False)
    flat_ids = my_part.reshape(-1)
    picks = (flat_ids[:, None] == jnp.arange(event_row_count, dtype=jnp.int32)[None, :]).astype(
        jnp.bfloat16
    )
    fetched = jnp.dot(picks, events, preferred_element_type=jnp.float32).astype(jnp.bfloat16)
    arrived_rows = lax.all_to_all(
        fetched.reshape(my_part.shape + (hidden_width,)), "ctx", split_axis=0, concat_axis=0, tiled=True
    )
    flat_rows = arrived_rows.reshape(ctx_size * slot_cap, hidden_width)
    return jnp.dot(
        own_hits.astype(jnp.bfloat16), flat_rows, preferred_element_type=jnp.float32
    ).astype(jnp.bfloat16)


def shards(events, w_in, w_out, rel_bias, lengths, block_lists, candidates):
    rows, width = events.shape
    heads = rel_bias.shape[0]
    users = lengths.shape[0]
    picks = block_lists.shape[1]
    count = lax.axis_size("ctx")
    my_index = lax.axis_index("ctx")
    total_rows = count * rows
    user_ends = jnp.cumsum(lengths)

    def times_of(block_num):
        return (
            block_num * rows + jnp.arange(rows, dtype=jnp.int32) + total_rows // 4
        ) % total_rows

    query_pos = times_of(my_index)
    query_user = user_of(query_pos, user_ends)
    lane = jnp.arange(PAIR, dtype=jnp.int32)[None, :] % (PAIR // 2)
    qm = jnp.where((lane == query_user[:, None]) | (lane > users), 0.0, NEG).astype(jnp.bfloat16)
    own_hot = (lane == query_user[:, None]).astype(jnp.bfloat16)

    table = jnp.asarray(BUFFER_OF, jnp.int32)[my_index % SPAN]
    infos, hots = [], []
    for p in range(picks):
        distance = block_lists[0, p]
        key_pos = times_of((my_index - distance) % count)
        key_user = user_of(key_pos, user_ends)
        useful = (key_pos[0] < query_pos[0]) & (key_user[rows - 1] >= query_user[0])
        infos.append(jnp.stack([table[distance - 1], distance, useful.astype(jnp.int32)]))
        hots.append((lane == key_user[:, None]).astype(jnp.bfloat16))
    info = jnp.stack(infos)
    hot = jnp.stack(hots)

    bufs = received(events, count)
    next_first = lax.ppermute(
        events[:1], "ctx", [((s + 1) % count, s) for s in range(count)]
    )
    following = jnp.concatenate([events[1:], next_first], axis=0)
    next_ok = (user_of(query_pos + 1, user_ends) == query_user) & (query_pos + 1 < total_rows)
    cand = fetch_candidates(events, candidates, count, my_index)

    vm = pl.BlockSpec(memory_space=pltpu.VMEM)
    sm = pl.BlockSpec(memory_space=pltpu.SMEM)
    hb = pl.BlockSpec(memory_space=pl.ANY)
    bf, f32 = jnp.bfloat16, jnp.float32
    gate, q, own = pl.pallas_call(
        first_kernel,
        out_shape=(
            jax.ShapeDtypeStruct((rows, width), bf),
            jax.ShapeDtypeStruct((rows, width), bf),
            jax.ShapeDtypeStruct((rows, width), f32),
        ),
        in_specs=[vm, hb, sm, vm, vm],
        out_specs=(vm, vm, vm),
        scratch_shapes=[
            pltpu.VMEM((4, width, width), bf),
            pltpu.VMEM((rows, width), bf),
            pltpu.VMEM((rows, width), bf),
            pltpu.VMEM((rows, width), bf),
            pltpu.VMEM((2, 2 * TILE, 4 * TILE), f32),
            pltpu.SemaphoreType.DMA((4,)),
        ],
        compiler_params=pltpu.CompilerParams(vmem_limit_bytes=VMEM_LIMIT),
        cost_estimate=pl.CostEstimate(
            flops=2 * rows * width * 4 * width + 4 * rows * rows * width,
            bytes_accessed=10 * width * width,
            transcendentals=heads * rows * rows,
        ),
        name="project_and_own_block",
    )(events, w_in, rel_bias, qm, own_hot)
    layer_output, next_score, scores = pl.pallas_call(
        second_kernel,
        out_shape=(
            jax.ShapeDtypeStruct((rows, width), bf),
            jax.ShapeDtypeStruct((rows, 1), f32),
            jax.ShapeDtypeStruct((rows, candidates.shape[1]), f32),
        ),
        in_specs=[sm, sm, vm, vm, vm, vm, vm, vm, vm, vm, vm, hb, hb] + [hb] * NBUF,
        out_specs=(vm, vm, vm),
        scratch_shapes=[
            pltpu.VMEM((picks, rows, width), bf),
            pltpu.VMEM((width, 2 * width), bf),
            pltpu.VMEM((width, width), bf),
            pltpu.VMEM((rows, width), bf),
            pltpu.VMEM((rows, 2 * width), bf),
            pltpu.VMEM((rows, width), f32),
            pltpu.VMEM((heads, 2 * TILE, 6 * TILE), f32),
            pltpu.SemaphoreType.DMA((picks + 2,)),
        ],
        compiler_params=pltpu.CompilerParams(vmem_limit_bytes=VMEM_LIMIT),
        cost_estimate=pl.CostEstimate(
            flops=2 * picks * (2 * rows * width * width + 2 * rows * rows * width),
            bytes_accessed=16 * width * width,
            transcendentals=2 * heads * rows * rows,
        ),
        name="earlier_blocks_and_output",
    )(
        info, rel_bias, events, gate, q, own, qm, hot, cand, following,
        next_ok.astype(f32)[:, None], w_in, w_out, *bufs,
    )
    return (layer_output, next_score[:, 0], scores)


def solution(mesh):
    in_specs = (
        P(("groups", "ctx"), None),
        P(),
        P(),
        P(),
        P("groups"),
        P(("groups", "ctx"), None),
        P("groups", None),
    )
    out_specs = (P(("groups", "ctx"), None), P(("groups", "ctx")), P(("groups", "ctx"), None))
    return jax.shard_map(shards, mesh=mesh, in_specs=in_specs, out_specs=out_specs, check_vma=False)
```

```python
import functools

import jax
import jax.numpy as jnp
from jax import lax
from jax.experimental import pallas as pl
from jax.experimental.pallas import tpu as pltpu
from jax.sharding import PartitionSpec as P

SPAN = 4
NEG = -1e30
TILE = 128
PAIR = 128
VMEM_LIMIT = 56 * 1024 * 1024
CHUNKS = 4
MESH = pl.DeviceIdType.MESH

NT = (((1,), (1,)), ((), ()))


def ends_of(lengths_ref):
    ends, total = [], 0
    for u in range(lengths_ref.shape[0]):
        total = total + lengths_ref[u]
        ends.append(total)
    return ends


def user_of(positions, ends):
    user = jnp.zeros_like(positions)
    for end in ends:
        user = user + (positions >= end).astype(jnp.int32)
    return user


def block_time(block, count):
    return lax.rem(block + count // 4, count)


def user_terms(time, rows, ends):
    row = lax.broadcasted_iota(jnp.int32, (rows, PAIR), 0)
    lane = lax.rem(lax.broadcasted_iota(jnp.int32, (rows, PAIR), 1), PAIR // 2)
    same = lane == user_of(time * rows + row, ends)
    one = jnp.where(same, 1.0, 0.0).astype(jnp.bfloat16)
    other = jnp.where(same, 0.0, NEG).astype(jnp.bfloat16)
    return other, one


def half_silu(u):
    return u * jnp.tanh(u) + u


def normalize(x):
    center = x - jnp.mean(x, -1, keepdims=True)
    spread = jnp.mean(center * center, -1, keepdims=True)
    return center * lax.rsqrt(spread + 1e-05)


def bucket_of(distance, buckets):
    return min(int(distance).bit_length(), buckets - 1) if distance > 0 else 0


def bias_tile(rel_ref, head, step, buckets):
    if step < 0:
        return jnp.full((TILE, TILE), NEG, jnp.float32)
    row = lax.broadcasted_iota(jnp.int32, (TILE, TILE), 0)
    col = lax.broadcasted_iota(jnp.int32, (TILE, TILE), 1)
    diff = row - col
    first = bucket_of(step * TILE - TILE + 1, buckets)
    last = bucket_of(step * TILE + TILE - 1, buckets)
    value = jnp.full((TILE, TILE), rel_ref[head, first] * 0.5, jnp.float32)
    for b in range(first + 1, last + 1):
        value = jnp.where(diff >= 2 ** (b - 1) - step * TILE, rel_ref[head, b] * 0.5, value)
    if step == 0:
        value = jnp.where(diff >= 0, value, NEG)
    return value


def fill_slab(slab, index, rel_ref, head, top, width, buckets):
    for step in range(top - width + 1, top + 2):
        tile = bias_tile(rel_ref, head, step, buckets)
        for a in range(2):
            p = top + a - step
            if 0 <= p < width:
                slab[index, a * TILE : (a + 1) * TILE, p * TILE : (p + 1) * TILE] = tile


def pair_operands(q, k, v, qm, hot):
    low = lax.broadcasted_iota(jnp.int32, (1, PAIR), 1) < PAIR // 2
    zero = jnp.zeros((), jnp.bfloat16)
    for side in range(2):
        mine = low if side == 0 else jnp.logical_not(low)
        yield (
            jnp.where(mine, q, qm),
            jnp.where(mine, k, hot),
            jnp.where(mine, v, zero),
        )


def first_kernel(
    count, x_ref, x_hbm, w_hbm, rel_ref, len_ref, gate_ref, q_ref, att_ref, recv, head_ref,
    w, normed, k_ref, v_ref, slab, qm_ref, hot_ref, sems, send_sem, recv_sem, head_sem,
):
    rows, width = x_ref.shape
    heads, buckets = rel_ref.shape
    piece = rows // CHUNKS
    me = lax.axis_index("ctx")
    place, plane = lax.rem(me, SPAN), me // SPAN
    planes = count // SPAN
    shift = planes // 4

    def flows(of):
        later = lax.rem(of + shift, planes) + 1
        return jnp.logical_and(later < planes, later != planes // 2)

    sends = flows(plane)
    fed = flows(lax.rem(plane + planes - 1, planes))
    odd = lax.rem(place, 2)
    low = place < 2
    ahead, behind = lax.rem(me + SPAN, count), lax.rem(me + count - SPAN, count)
    after, before = lax.rem(me + 1, count), lax.rem(me + count - 1, count)
    beside = me + 1 - 2 * odd
    opposite = jnp.where(low, me + 2, me - 2)
    relayed = jnp.logical_or(place >= 2, fed)

    barrier = pltpu.get_barrier_semaphore()
    for other in (after, before, beside, opposite):
        pl.semaphore_signal(barrier, inc=1, device_id={"ctx": other}, device_id_type=MESH)

    @pl.when(sends)
    def _():
        pl.semaphore_signal(barrier, inc=1, device_id={"ctx": ahead}, device_id_type=MESH)

    @pl.when(fed)
    def _():
        pl.semaphore_signal(barrier, inc=1, device_id={"ctx": behind}, device_id_type=MESH)

    pl.semaphore_wait(barrier, 4 + sends.astype(jnp.int32) + fed.astype(jnp.int32))

    def part(c):
        return pl.ds(c * piece, piece)

    kinds = {
        0: (sends, None, 3, ahead),
        1: (low, None, 1, opposite),
        2: (odd == 0, None, 0, beside),
        3: (jnp.logical_and(place >= 2, fed), 3, 1, opposite),
        4: (jnp.logical_and(odd == 1, fed), 3, 2, beside),
        5: (jnp.logical_and(relayed, odd == 0), 1, 2, beside),
        6: (jnp.logical_and(relayed, odd == 1), 1, 0, beside),
    }

    def sending(kind, c):
        _, source, slot, to = kinds[kind]
        return pltpu.make_async_remote_copy(
            src_ref=x_hbm.at[part(c)] if source is None else recv.at[source, part(c)],
            dst_ref=recv.at[slot, part(c)],
            send_sem=send_sem.at[kind, c],
            recv_sem=recv_sem.at[slot, c],
            device_id={"ctx": to},
            device_id_type=MESH,
        )

    def start(kind, c):
        @pl.when(kinds[kind][0])
        def _():
            sending(kind, c).start()

    def arrived(slot, c, when):
        @pl.when(when)
        def _():
            pltpu.make_async_copy(
                recv.at[slot, part(c)], recv.at[slot, part(c)], recv_sem.at[slot, c]
            ).wait()

    def earlier(c):
        arrived(3, c, fed)
        start(3, c)
        start(4, c)

    def relay(c):
        arrived(1, c, relayed)
        start(5, c)
        start(6, c)

    for c in range(CHUNKS):
        start(0, c)
        start(1, c)
    for c in range(CHUNKS):
        start(2, c)
    heading = pltpu.make_async_remote_copy(
        src_ref=x_hbm.at[pl.ds(0, 16)],
        dst_ref=head_ref,
        send_sem=head_sem.at[0],
        recv_sem=head_sem.at[1],
        device_id={"ctx": before},
        device_id_type=MESH,
    )
    heading.start()
    order = (1, 3, 2, 0)
    copies = {
        g: pltpu.make_async_copy(
            w_hbm.at[:, g * width : (g + 1) * width], w.at[g], sems.at[g]
        )
        for g in order
    }
    for g in order:
        copies[g].start()
    normed[...] = normalize(x_ref[...].astype(jnp.float32)).astype(jnp.bfloat16)
    qm_ref[...], hot_ref[...] = user_terms(block_time(me, count), rows, ends_of(len_ref))

    def project(g, out, scale):
        def step(j, carry):
            cols = pl.ds(pl.multiple_of(j * 256, 256), 256)
            u = 0.5 * jnp.dot(normed[...], w[g, :, cols], preferred_element_type=jnp.float32)
            y = half_silu(u).astype(jnp.bfloat16)
            out[:, cols] = y if scale is None else y * jnp.asarray(scale, jnp.bfloat16)
            return carry

        copies[g].wait()
        lax.fori_loop(0, width // 256, step, 0)

    project(1, q_ref, 0.5 * (width // heads) ** -0.5)
    project(3, k_ref, None)
    project(2, v_ref, None)
    earlier(0)
    project(0, gate_ref, None)
    earlier(1)

    half = rows // 2

    def pair(hp, carry):
        cols = pl.ds(pl.multiple_of(hp * PAIR, PAIR), PAIR)
        for side in range(2):
            fill_slab(slab, side, rel_ref, 2 * hp + side, 2, 4, buckets)
        tops = []
        for side, (q, k, v) in enumerate(
            pair_operands(q_ref[:, cols], k_ref[:, cols], v_ref[:, cols], qm_ref[...], hot_ref[...])
        ):
            s0 = lax.dot_general(q[:half], k[:half], NT, preferred_element_type=jnp.float32)
            s1 = lax.dot_general(q[half:], k, NT, preferred_element_type=jnp.float32)
            w0 = half_silu(s0 + slab[side, :, half:]).astype(jnp.bfloat16)
            w1 = half_silu(s1 + slab[side]).astype(jnp.bfloat16)
            tops.append(
                (
                    jnp.dot(w0, v[:half], preferred_element_type=jnp.float32),
                    jnp.dot(w1, v, preferred_element_type=jnp.float32),
                )
            )
        att_ref[:half, cols] = tops[0][0] + tops[1][0]
        att_ref[half:, cols] = tops[0][1] + tops[1][1]
        return carry

    lax.fori_loop(0, heads // 4, pair, 0)
    relay(0)
    earlier(2)
    lax.fori_loop(heads // 4, heads // 2, pair, 0)
    relay(1)
    earlier(3)
    relay(2)
    relay(3)
    for c in range(CHUNKS):
        arrived(0, c, jnp.logical_or(odd == 1, relayed))
        arrived(2, c, jnp.logical_or(place == 3, fed))
        for kind in kinds:
            @pl.when(kinds[kind][0])
            def _(kind=kind, c=c):
                sending(kind, c).wait_send()
    heading.wait()


def second_kernel(
    count, list_ref, len_ref, rel_ref, x_ref, gate_ref, q_ref, own_ref, head_ref, cand_ref,
    w_hbm, wout_hbm, recv, out_ref, next_ref, table_ref,
    picked, wkv, wout, normed, kv, att, slab, qm_ref, hot_ref, follow, sems,
):
    rows, width = x_ref.shape
    heads, buckets = rel_ref.shape
    picks = list_ref.shape[1]
    half = rows // 2
    ends = ends_of(len_ref)
    time = block_time(lax.axis_index("ctx"), count)
    useful = []
    for p in range(picks):
        distance = list_ref[0, p]
        last = (time - distance + 1) * rows - 1
        useful.append((distance <= time) & (user_of(last, ends) >= user_of(time * rows, ends)))

        @pl.when(useful[p])
        def _(p=p, distance=distance):
            pltpu.make_async_copy(recv.at[distance - 1], picked.at[p], sems.at[p]).start()
    w_copy = pltpu.make_async_copy(w_hbm.at[:, 2 * width :], wkv, sems.at[picks])
    o_copy = pltpu.make_async_copy(wout_hbm, wout, sems.at[picks + 1])
    w_copy.start()
    o_copy.start()
    att[...] = own_ref[...]
    qm_ref[...] = user_terms(time, rows, ends)[0]
    w_copy.wait()
    for p in range(picks):
        @pl.when(useful[p])
        def _(p=p):
            distance = list_ref[0, p]
            pltpu.make_async_copy(recv.at[0], picked.at[p], sems.at[p]).wait()
            hot_ref[...] = user_terms(time - distance, rows, ends)[1]
            normed[...] = normalize(picked[p].astype(jnp.float32)).astype(jnp.bfloat16)

            def step(j, carry):
                cols = pl.ds(pl.multiple_of(j * 256, 256), 256)
                u = 0.5 * jnp.dot(normed[...], wkv[:, cols], preferred_element_type=jnp.float32)
                kv[:, cols] = half_silu(u).astype(jnp.bfloat16)
                return carry

            lax.fori_loop(0, 2 * width // 256, step, 0)
            for d in range(1, SPAN + 1):
                @pl.when(distance == d)
                def _(d=d):
                    def fill(h, carry):
                        fill_slab(slab, h, rel_ref, h, (rows // TILE) * d + 2, 6, buckets)
                        return carry

                    lax.fori_loop(0, heads, fill, 0)

            def pair(hp, carry):
                cols = pl.ds(pl.multiple_of(hp * PAIR, PAIR), PAIR)
                kcols = pl.ds(pl.multiple_of(width + hp * PAIR, PAIR), PAIR)
                tops = []
                for side, (q, k, v) in enumerate(
                    pair_operands(q_ref[:, cols], kv[:, kcols], kv[:, cols], qm_ref[...], hot_ref[...])
                ):
                    h = 2 * hp + side
                    s0 = lax.dot_general(q[:half], k, NT, preferred_element_type=jnp.float32)
                    s1 = lax.dot_general(q[half:], k, NT, preferred_element_type=jnp.float32)
                    w0 = half_silu(s0 + slab[h, :, half:]).astype(jnp.bfloat16)
                    w1 = half_silu(s1 + slab[h, :, :rows]).astype(jnp.bfloat16)
                    tops.append(
                        (
                            jnp.dot(w0, v, preferred_element_type=jnp.float32),
                            jnp.dot(w1, v, preferred_element_type=jnp.float32),
                        )
                    )
                att[:half, cols] += tops[0][0] + tops[1][0]
                att[half:, cols] += tops[0][1] + tops[1][1]
                return carry

            lax.fori_loop(0, heads // 2, pair, 0)
    o_copy.wait()
    scale = width**-0.5
    last_row = lax.broadcasted_iota(jnp.int32, (rows, 1), 0) == rows - 1
    follow[...] = jnp.where(
        last_row,
        head_ref[0:1, :].astype(jnp.float32),
        pltpu.roll(x_ref[...].astype(jnp.float32), rows - 1, 0),
    )

    def finish(r, carry):
        rs = pl.ds(pl.multiple_of(r * 256, 256), 256)
        gated = (normalize(att[rs, :]) * gate_ref[rs, :].astype(jnp.float32)).astype(jnp.bfloat16)
        added = jnp.dot(gated, wout[...], preferred_element_type=jnp.float32)
        layer = (x_ref[rs, :].astype(jnp.float32) + added).astype(jnp.bfloat16)
        out_ref[rs, :] = layer
        inner = jnp.sum(
            layer.astype(jnp.float32) * follow[rs, :], axis=1, keepdims=True
        )
        at = time * rows + r * 256 + lax.broadcasted_iota(jnp.int32, (256, 1), 0)
        same = (user_of(at + 1, ends) == user_of(at, ends)) & (at + 1 < count * rows)
        next_ref[rs, :] = jnp.where(same, inner * scale, 0.0)
        table_ref[rs, :] = (
            lax.dot_general(layer, cand_ref[...], NT, preferred_element_type=jnp.float32) * scale
        )
        return carry

    lax.fori_loop(0, rows // 256, finish, 0)


def fetch_candidates(events, candidates, ctx_size, my_index):
    event_row_count, hidden_width = events.shape
    cand_count = candidates.shape[1]
    slot_cap = 2 * cand_count // ctx_size
    number = jnp.arange(cand_count, dtype=jnp.int32)
    before = number[:, None] < number[None, :]
    mine = candidates // event_row_count == my_index
    rank = jnp.dot(
        mine.astype(jnp.bfloat16), before.astype(jnp.bfloat16), preferred_element_type=jnp.float32
    ).astype(jnp.int32)
    local = jnp.where(mine, candidates % event_row_count, -1)
    slots = jnp.arange(slot_cap, dtype=jnp.int32)
    ids = jnp.max(
        jnp.where(rank[:, None, :] == slots[None, :, None], local[:, None, :], -1), axis=2
    ).reshape(-1)
    picks = (ids[:, None] == jnp.arange(event_row_count, dtype=jnp.int32)[None, :]).astype(jnp.bfloat16)
    fetched = jnp.dot(picks, events, preferred_element_type=jnp.float32).astype(jnp.bfloat16)
    arrived_rows = lax.all_to_all(
        fetched.reshape(ctx_size, slot_cap, hidden_width), "ctx", split_axis=0, concat_axis=0, tiled=True
    )
    owner = lax.dynamic_slice_in_dim(candidates, my_index, 1, 0)[0] // event_row_count
    own_rank = jnp.sum(
        ((owner[:, None] == owner[None, :]) & before.T).astype(jnp.int32), axis=1
    )
    own_slot = owner * slot_cap + own_rank
    own_hits = own_slot[:, None] == jnp.arange(ctx_size * slot_cap, dtype=jnp.int32)[None, :]
    return jnp.dot(
        own_hits.astype(jnp.bfloat16),
        arrived_rows.reshape(ctx_size * slot_cap, hidden_width),
        preferred_element_type=jnp.float32,
    ).astype(jnp.bfloat16)


def shards(events, w_in, w_out, rel_bias, lengths, block_lists, candidates):
    rows, width = events.shape
    heads = rel_bias.shape[0]
    picks = block_lists.shape[1]
    count = lax.axis_size("ctx")
    cand = fetch_candidates(events, candidates, count, lax.axis_index("ctx"))

    vm = pl.BlockSpec(memory_space=pltpu.VMEM)
    sm = pl.BlockSpec(memory_space=pltpu.SMEM)
    hb = pl.BlockSpec(memory_space=pl.ANY)
    bf, f32 = jnp.bfloat16, jnp.float32
    gate, q, own, recv, following = pl.pallas_call(
        functools.partial(first_kernel, count),
        out_shape=(
            jax.ShapeDtypeStruct((rows, width), bf),
            jax.ShapeDtypeStruct((rows, width), bf),
            jax.ShapeDtypeStruct((rows, width), f32),
            jax.ShapeDtypeStruct((SPAN, rows, width), bf),
            jax.ShapeDtypeStruct((16, width), bf),
        ),
        in_specs=[vm, hb, hb, sm, sm],
        out_specs=(vm, vm, vm, hb, hb),
        scratch_shapes=[
            pltpu.VMEM((4, width, width), bf),
            pltpu.VMEM((rows, width), bf),
            pltpu.VMEM((rows, width), bf),
            pltpu.VMEM((rows, width), bf),
            pltpu.VMEM((2, 2 * TILE, 4 * TILE), f32),
            pltpu.VMEM((rows, PAIR), bf),
            pltpu.VMEM((rows, PAIR), bf),
            pltpu.SemaphoreType.DMA((4,)),
            pltpu.SemaphoreType.DMA((7, CHUNKS)),
            pltpu.SemaphoreType.DMA((SPAN, CHUNKS)),
            pltpu.SemaphoreType.DMA((2,)),
        ],
        compiler_params=pltpu.CompilerParams(
            vmem_limit_bytes=VMEM_LIMIT, collective_id=0, has_side_effects=True
        ),
        cost_estimate=pl.CostEstimate(
            flops=2 * rows * width * 4 * width + 4 * rows * rows * width,
            bytes_accessed=10 * width * width,
            transcendentals=heads * rows * rows,
        ),
        name="project_and_own_block",
    )(events, events, w_in, rel_bias, lengths)
    layer_output, next_score, scores = pl.pallas_call(
        functools.partial(second_kernel, count),
        out_shape=(
            jax.ShapeDtypeStruct((rows, width), bf),
            jax.ShapeDtypeStruct((rows, 1), f32),
            jax.ShapeDtypeStruct((rows, candidates.shape[1]), f32),
        ),
        in_specs=[sm, sm, sm, vm, vm, vm, vm, vm, vm, hb, hb, hb],
        out_specs=(vm, vm, vm),
        scratch_shapes=[
            pltpu.VMEM((picks, rows, width), bf),
            pltpu.VMEM((width, 2 * width), bf),
            pltpu.VMEM((width, width), bf),
            pltpu.VMEM((rows, width), bf),
            pltpu.VMEM((rows, 2 * width), bf),
            pltpu.VMEM((rows, width), f32),
            pltpu.VMEM((heads, 2 * TILE, 6 * TILE), f32),
            pltpu.VMEM((rows, PAIR), bf),
            pltpu.VMEM((rows, PAIR), bf),
            pltpu.VMEM((rows, width), f32),
            pltpu.SemaphoreType.DMA((picks + 2,)),
        ],
        compiler_params=pltpu.CompilerParams(vmem_limit_bytes=VMEM_LIMIT),
        cost_estimate=pl.CostEstimate(
            flops=2 * picks * (2 * rows * width * width + 2 * rows * rows * width),
            bytes_accessed=16 * width * width,
            transcendentals=2 * heads * rows * rows,
        ),
        name="earlier_blocks_and_output",
    )(
        block_lists, lengths, rel_bias, events, gate, q, own, following, cand, w_in, w_out, recv,
    )
    return (layer_output, next_score[:, 0], scores)


def solution(mesh):
    in_specs = (
        P(("groups", "ctx"), None),
        P(),
        P(),
        P(),
        P("groups"),
        P(("groups", "ctx"), None),
        P("groups", None),
    )
    out_specs = (P(("groups", "ctx"), None), P(("groups", "ctx")), P(("groups", "ctx"), None))
    return jax.shard_map(shards, mesh=mesh, in_specs=in_specs, out_specs=out_specs, check_vma=False)
```

```python
import functools

import jax
import jax.numpy as jnp
from jax import lax
from jax.experimental import pallas as pl
from jax.experimental.pallas import tpu as pltpu
from jax.sharding import PartitionSpec as P

SPAN = 4
NEG = -1e30
TILE = 128
PAIR = 128
VMEM_LIMIT = 56 * 1024 * 1024
CHUNKS = 8
MESH = pl.DeviceIdType.MESH

NT = (((1,), (1,)), ((), ()))


def ends_of(lengths_ref):
    ends, total = [], 0
    for u in range(lengths_ref.shape[0]):
        total = total + lengths_ref[u]
        ends.append(total)
    return ends


def user_of(positions, ends):
    user = jnp.zeros_like(positions)
    for end in ends:
        user = user + (positions >= end).astype(jnp.int32)
    return user


def block_time(block, count):
    return lax.rem(block + count // 4, count)


def user_terms(time, rows, ends):
    row = lax.broadcasted_iota(jnp.int32, (rows, PAIR), 0)
    lane = lax.rem(lax.broadcasted_iota(jnp.int32, (rows, PAIR), 1), PAIR // 2)
    same = lane == user_of(time * rows + row, ends)
    one = jnp.where(same, 1.0, 0.0).astype(jnp.bfloat16)
    other = jnp.where(same, 0.0, NEG).astype(jnp.bfloat16)
    return other, one


def half_silu(u):
    return u * jnp.tanh(u) + u


def normalize(x):
    center = x - jnp.mean(x, -1, keepdims=True)
    spread = jnp.mean(center * center, -1, keepdims=True)
    return center * lax.rsqrt(spread + 1e-05)


def bucket_of(distance, buckets):
    return min(int(distance).bit_length(), buckets - 1) if distance > 0 else 0


def bias_tile(rel_ref, head, step, buckets):
    if step < 0:
        return jnp.full((TILE, TILE), NEG, jnp.float32)
    row = lax.broadcasted_iota(jnp.int32, (TILE, TILE), 0)
    col = lax.broadcasted_iota(jnp.int32, (TILE, TILE), 1)
    diff = row - col
    first = bucket_of(step * TILE - TILE + 1, buckets)
    last = bucket_of(step * TILE + TILE - 1, buckets)
    value = jnp.full((TILE, TILE), rel_ref[head, first] * 0.5, jnp.float32)
    for b in range(first + 1, last + 1):
        value = jnp.where(diff >= 2 ** (b - 1) - step * TILE, rel_ref[head, b] * 0.5, value)
    if step == 0:
        value = jnp.where(diff >= 0, value, NEG)
    return value


def fill_slab(slab, index, rel_ref, head, top, width, buckets):
    for step in range(top - width + 1, top + 2):
        tile = bias_tile(rel_ref, head, step, buckets)
        for a in range(2):
            p = top + a - step
            if 0 <= p < width:
                slab[index, a * TILE : (a + 1) * TILE, p * TILE : (p + 1) * TILE] = tile


def pair_operands(q, k, v, qm, hot):
    low = lax.broadcasted_iota(jnp.int32, (1, PAIR), 1) < PAIR // 2
    zero = jnp.zeros((), jnp.bfloat16)
    for side in range(2):
        mine = low if side == 0 else jnp.logical_not(low)
        yield (
            jnp.where(mine, q, qm),
            jnp.where(mine, k, hot),
            jnp.where(mine, v, zero),
        )


def first_kernel(
    count, x_ref, x_hbm, w_hbm, rel_ref, len_ref, picks_ref, gate_ref, q_ref, att_ref, recv, head_ref, cand_recv,
    w, normed, k_ref, v_ref, slab, qm_ref, hot_ref, fetched, sems, send_sem, recv_sem, head_sem, cand_send, cand_sem,
):
    rows, width = x_ref.shape
    heads, buckets = rel_ref.shape
    piece = rows // CHUNKS
    me = lax.axis_index("ctx")
    place, plane = lax.rem(me, SPAN), me // SPAN
    planes = count // SPAN
    shift = planes // 4

    def flows(of):
        later = lax.rem(of + shift, planes) + 1
        return jnp.logical_and(later < planes, later != planes // 2)

    sends = flows(plane)
    fed = flows(lax.rem(plane + planes - 1, planes))
    odd = lax.rem(place, 2)
    low = place < 2
    ahead = lax.rem(me + SPAN, count)
    before = lax.rem(me + count - 1, count)
    beside = me + 1 - 2 * odd
    opposite = jnp.where(low, me + 2, me - 2)
    relayed = jnp.logical_or(place >= 2, fed)

    barrier = pltpu.get_barrier_semaphore()

    def greet(j, carry):
        other = lax.rem(me + j, count)
        pl.semaphore_signal(barrier, inc=1, device_id={"ctx": other}, device_id_type=MESH)
        return carry

    lax.fori_loop(1, count, greet, 0)
    pl.semaphore_wait(barrier, count - 1)

    def part(c):
        return pl.ds(c * piece, piece)

    kinds = {
        0: (sends, None, 3, ahead),
        1: (low, None, 1, opposite),
        2: (odd == 0, None, 0, beside),
        3: (jnp.logical_and(place >= 2, fed), 3, 1, opposite),
        4: (jnp.logical_and(odd == 1, fed), 3, 2, beside),
        5: (jnp.logical_and(relayed, odd == 0), 1, 2, beside),
        6: (jnp.logical_and(relayed, odd == 1), 1, 0, beside),
    }

    def sending(kind, c):
        _, source, slot, to = kinds[kind]
        return pltpu.make_async_remote_copy(
            src_ref=x_hbm.at[part(c)] if source is None else recv.at[source, part(c)],
            dst_ref=recv.at[slot, part(c)],
            send_sem=send_sem.at[kind, c],
            recv_sem=recv_sem.at[slot, c],
            device_id={"ctx": to},
            device_id_type=MESH,
        )

    def start(kind, c):
        @pl.when(kinds[kind][0])
        def _():
            sending(kind, c).start()

    def arrived(slot, c, when):
        @pl.when(when)
        def _():
            pltpu.make_async_copy(
                recv.at[slot, part(c)], recv.at[slot, part(c)], recv_sem.at[slot, c]
            ).wait()

    def earlier(c):
        arrived(3, c, fed)
        start(3, c)
        start(4, c)

    def relay(c):
        arrived(1, c, relayed)
        start(5, c)
        start(6, c)

    for c in range(CHUNKS):
        start(0, c)
        start(1, c)
    for c in range(CHUNKS):
        start(2, c)
    heading = pltpu.make_async_remote_copy(
        src_ref=x_hbm.at[pl.ds(0, 16)],
        dst_ref=head_ref,
        send_sem=head_sem.at[0],
        recv_sem=head_sem.at[1],
        device_id={"ctx": before},
        device_id_type=MESH,
    )
    heading.start()
    cap = picks_ref.shape[0] // count
    fetched[...] = (
        jnp.dot(picks_ref[...], x_ref[...], preferred_element_type=jnp.float32)
        .astype(jnp.bfloat16)
        .reshape(count, cap, width)
    )

    def candidate(j):
        to = lax.rem(me + j, count)
        return pltpu.make_async_remote_copy(
            src_ref=fetched.at[to],
            dst_ref=cand_recv.at[me],
            send_sem=cand_send.at[j],
            recv_sem=cand_sem.at[me],
            device_id={"ctx": to},
            device_id_type=MESH,
        )

    def send_candidate(j, carry):
        candidate(j).start()
        return carry

    lax.fori_loop(1, count, send_candidate, 0)
    own_rows = pltpu.make_async_copy(fetched.at[me], cand_recv.at[me], cand_send.at[0])
    own_rows.start()
    order = (1, 3, 2, 0)
    copies = {
        g: pltpu.make_async_copy(
            w_hbm.at[:, g * width : (g + 1) * width], w.at[g], sems.at[g]
        )
        for g in order
    }
    for g in order:
        copies[g].start()
    normed[...] = normalize(x_ref[...].astype(jnp.float32)).astype(jnp.bfloat16)
    qm_ref[...], hot_ref[...] = user_terms(block_time(me, count), rows, ends_of(len_ref))

    def project(g, out, scale):
        def step(j, carry):
            cols = pl.ds(pl.multiple_of(j * 256, 256), 256)
            u = 0.5 * jnp.dot(normed[...], w[g, :, cols], preferred_element_type=jnp.float32)
            y = half_silu(u).astype(jnp.bfloat16)
            out[:, cols] = y if scale is None else y * jnp.asarray(scale, jnp.bfloat16)
            return carry

        copies[g].wait()
        lax.fori_loop(0, width // 256, step, 0)

    project(1, q_ref, 0.5 * (width // heads) ** -0.5)
    project(3, k_ref, None)
    project(2, v_ref, None)
    earlier(0)
    project(0, gate_ref, None)
    earlier(1)

    half = rows // 2

    def pair(hp, carry):
        cols = pl.ds(pl.multiple_of(hp * PAIR, PAIR), PAIR)
        for side in range(2):
            fill_slab(slab, side, rel_ref, 2 * hp + side, 2, 4, buckets)
        tops = []
        for side, (q, k, v) in enumerate(
            pair_operands(q_ref[:, cols], k_ref[:, cols], v_ref[:, cols], qm_ref[...], hot_ref[...])
        ):
            s0 = lax.dot_general(q[:half], k[:half], NT, preferred_element_type=jnp.float32)
            s1 = lax.dot_general(q[half:], k, NT, preferred_element_type=jnp.float32)
            w0 = half_silu(s0 + slab[side, :, half:]).astype(jnp.bfloat16)
            w1 = half_silu(s1 + slab[side]).astype(jnp.bfloat16)
            tops.append(
                (
                    jnp.dot(w0, v[:half], preferred_element_type=jnp.float32),
                    jnp.dot(w1, v, preferred_element_type=jnp.float32),
                )
            )
        att_ref[:half, cols] = tops[0][0] + tops[1][0]
        att_ref[half:, cols] = tops[0][1] + tops[1][1]
        return carry

    pairs = heads // 2
    lax.fori_loop(0, pairs // 4, pair, 0)
    earlier(2)
    relay(0)
    lax.fori_loop(pairs // 4, pairs * 5 // 8, pair, 0)
    earlier(3)
    relay(1)
    lax.fori_loop(pairs * 5 // 8, pairs, pair, 0)
    for c in range(4, CHUNKS):
        earlier(c)
        relay(c - 2)
    relay(CHUNKS - 2)
    relay(CHUNKS - 1)

    def end_candidate(j, carry):
        source = lax.rem(me + j, count)
        pltpu.make_async_copy(
            cand_recv.at[source], cand_recv.at[source], cand_sem.at[source]
        ).wait()
        candidate(j).wait_send()
        return carry

    own_rows.wait()
    lax.fori_loop(1, count, end_candidate, 0)
    for c in range(CHUNKS):
        arrived(0, c, jnp.logical_or(odd == 1, relayed))
        arrived(2, c, jnp.logical_or(place == 3, fed))
        for kind in kinds:
            @pl.when(kinds[kind][0])
            def _(kind=kind, c=c):
                sending(kind, c).wait_send()
    heading.wait()


def second_kernel(
    count, list_ref, len_ref, rel_ref, x_ref, gate_ref, q_ref, own_ref, head_ref, cand_ref,
    w_hbm, wout_hbm, recv, out_ref, next_ref, table_ref,
    picked, wkv, wout, normed, kv, att, slab, qm_ref, hot_ref, follow, sems,
):
    rows, width = x_ref.shape
    heads, buckets = rel_ref.shape
    picks = list_ref.shape[1]
    half = rows // 2
    ends = ends_of(len_ref)
    time = block_time(lax.axis_index("ctx"), count)
    useful = []
    for p in range(picks):
        distance = list_ref[0, p]
        last = (time - distance + 1) * rows - 1
        useful.append((distance <= time) & (user_of(last, ends) >= user_of(time * rows, ends)))

        @pl.when(useful[p])
        def _(p=p, distance=distance):
            pltpu.make_async_copy(recv.at[distance - 1], picked.at[p], sems.at[p]).start()
    w_copy = pltpu.make_async_copy(w_hbm.at[:, 2 * width :], wkv, sems.at[picks])
    o_copy = pltpu.make_async_copy(wout_hbm, wout, sems.at[picks + 1])
    w_copy.start()
    o_copy.start()
    att[...] = own_ref[...]
    qm_ref[...] = user_terms(time, rows, ends)[0]
    w_copy.wait()
    for p in range(picks):
        @pl.when(useful[p])
        def _(p=p):
            distance = list_ref[0, p]
            pltpu.make_async_copy(recv.at[0], picked.at[p], sems.at[p]).wait()
            hot_ref[...] = user_terms(time - distance, rows, ends)[1]
            normed[...] = normalize(picked[p].astype(jnp.float32)).astype(jnp.bfloat16)

            def step(j, carry):
                cols = pl.ds(pl.multiple_of(j * 256, 256), 256)
                u = 0.5 * jnp.dot(normed[...], wkv[:, cols], preferred_element_type=jnp.float32)
                kv[:, cols] = half_silu(u).astype(jnp.bfloat16)
                return carry

            lax.fori_loop(0, 2 * width // 256, step, 0)
            for d in range(1, SPAN + 1):
                @pl.when(distance == d)
                def _(d=d):
                    def fill(h, carry):
                        fill_slab(slab, h, rel_ref, h, (rows // TILE) * d + 2, 6, buckets)
                        return carry

                    lax.fori_loop(0, heads, fill, 0)

            def pair(hp, carry):
                cols = pl.ds(pl.multiple_of(hp * PAIR, PAIR), PAIR)
                kcols = pl.ds(pl.multiple_of(width + hp * PAIR, PAIR), PAIR)
                tops = []
                for side, (q, k, v) in enumerate(
                    pair_operands(q_ref[:, cols], kv[:, kcols], kv[:, cols], qm_ref[...], hot_ref[...])
                ):
                    h = 2 * hp + side
                    s0 = lax.dot_general(q[:half], k, NT, preferred_element_type=jnp.float32)
                    s1 = lax.dot_general(q[half:], k, NT, preferred_element_type=jnp.float32)
                    w0 = half_silu(s0 + slab[h, :, half:]).astype(jnp.bfloat16)
                    w1 = half_silu(s1 + slab[h, :, :rows]).astype(jnp.bfloat16)
                    tops.append(
                        (
                            jnp.dot(w0, v, preferred_element_type=jnp.float32),
                            jnp.dot(w1, v, preferred_element_type=jnp.float32),
                        )
                    )
                att[:half, cols] += tops[0][0] + tops[1][0]
                att[half:, cols] += tops[0][1] + tops[1][1]
                return carry

            lax.fori_loop(0, heads // 2, pair, 0)
    o_copy.wait()
    scale = width**-0.5
    last_row = lax.broadcasted_iota(jnp.int32, (rows, 1), 0) == rows - 1
    follow[...] = jnp.where(
        last_row,
        head_ref[0:1, :].astype(jnp.float32),
        pltpu.roll(x_ref[...].astype(jnp.float32), rows - 1, 0),
    )

    def finish(r, carry):
        rs = pl.ds(pl.multiple_of(r * 256, 256), 256)
        gated = (normalize(att[rs, :]) * gate_ref[rs, :].astype(jnp.float32)).astype(jnp.bfloat16)
        added = jnp.dot(gated, wout[...], preferred_element_type=jnp.float32)
        layer = (x_ref[rs, :].astype(jnp.float32) + added).astype(jnp.bfloat16)
        out_ref[rs, :] = layer
        inner = jnp.sum(
            layer.astype(jnp.float32) * follow[rs, :], axis=1, keepdims=True
        )
        at = time * rows + r * 256 + lax.broadcasted_iota(jnp.int32, (256, 1), 0)
        same = (user_of(at + 1, ends) == user_of(at, ends)) & (at + 1 < count * rows)
        score = jnp.where(same, inner * scale, 0.0)
        eye = lax.broadcasted_iota(jnp.int32, (TILE, TILE), 0) == lax.broadcasted_iota(
            jnp.int32, (TILE, TILE), 1
        )
        for j in range(256 // TILE):
            spread = jnp.where(eye, score[j * TILE : (j + 1) * TILE], 0.0)
            next_ref[r * (256 // TILE) + j] = jnp.sum(spread, axis=0, keepdims=True)
        table_ref[rs, :] = (
            lax.dot_general(layer, cand_ref[...], NT, preferred_element_type=jnp.float32) * scale
        )
        return carry

    lax.fori_loop(0, rows // 256, finish, 0)


def candidate_slots(candidates, event_row_count, ctx_size, my_index):
    cand_count = candidates.shape[1]
    slot_cap = max(2 * cand_count // ctx_size, 16)
    number = jnp.arange(cand_count, dtype=jnp.int32)
    before = number[:, None] < number[None, :]
    mine = candidates // event_row_count == my_index
    rank = jnp.dot(
        mine.astype(jnp.bfloat16), before.astype(jnp.bfloat16), preferred_element_type=jnp.float32
    ).astype(jnp.int32)
    local = jnp.where(mine, candidates % event_row_count, -1)
    slots = jnp.arange(slot_cap, dtype=jnp.int32)
    ids = jnp.max(
        jnp.where(rank[:, None, :] == slots[None, :, None], local[:, None, :], -1), axis=2
    ).reshape(-1)
    picks = (ids[:, None] == jnp.arange(event_row_count, dtype=jnp.int32)[None, :]).astype(jnp.bfloat16)
    owner = lax.dynamic_slice_in_dim(candidates, my_index, 1, 0)[0] // event_row_count
    own_rank = jnp.sum(
        ((owner[:, None] == owner[None, :]) & before.T).astype(jnp.int32), axis=1
    )
    own_slot = owner * slot_cap + own_rank
    own_hits = own_slot[:, None] == jnp.arange(ctx_size * slot_cap, dtype=jnp.int32)[None, :]
    return picks, own_hits.astype(jnp.bfloat16)


def shards(events, w_in, w_out, rel_bias, lengths, block_lists, candidates):
    rows, width = events.shape
    heads = rel_bias.shape[0]
    picks = block_lists.shape[1]
    count = lax.axis_size("ctx")
    asked, own_hits = candidate_slots(candidates, rows, count, lax.axis_index("ctx"))
    cap = asked.shape[0] // count

    vm = pl.BlockSpec(memory_space=pltpu.VMEM)
    sm = pl.BlockSpec(memory_space=pltpu.SMEM)
    hb = pl.BlockSpec(memory_space=pl.ANY)
    bf, f32 = jnp.bfloat16, jnp.float32
    gate, q, own, recv, following, arrived_rows = pl.pallas_call(
        functools.partial(first_kernel, count),
        out_shape=(
            jax.ShapeDtypeStruct((rows, width), bf),
            jax.ShapeDtypeStruct((rows, width), bf),
            jax.ShapeDtypeStruct((rows, width), f32),
            jax.ShapeDtypeStruct((SPAN, rows, width), bf),
            jax.ShapeDtypeStruct((16, width), bf),
            jax.ShapeDtypeStruct((count, cap, width), bf),
        ),
        in_specs=[vm, hb, hb, sm, sm, vm],
        out_specs=(vm, vm, vm, hb, hb, hb),
        scratch_shapes=[
            pltpu.VMEM((4, width, width), bf),
            pltpu.VMEM((rows, width), bf),
            pltpu.VMEM((rows, width), bf),
            pltpu.VMEM((rows, width), bf),
            pltpu.VMEM((2, 2 * TILE, 4 * TILE), f32),
            pltpu.VMEM((rows, PAIR), bf),
            pltpu.VMEM((rows, PAIR), bf),
            pltpu.VMEM((count, cap, width), bf),
            pltpu.SemaphoreType.DMA((4,)),
            pltpu.SemaphoreType.DMA((7, CHUNKS)),
            pltpu.SemaphoreType.DMA((SPAN, CHUNKS)),
            pltpu.SemaphoreType.DMA((2,)),
            pltpu.SemaphoreType.DMA((count,)),
            pltpu.SemaphoreType.DMA((count,)),
        ],
        compiler_params=pltpu.CompilerParams(
            vmem_limit_bytes=VMEM_LIMIT, collective_id=0, has_side_effects=True
        ),
        cost_estimate=pl.CostEstimate(
            flops=2 * rows * width * 4 * width + 4 * rows * rows * width,
            bytes_accessed=10 * width * width,
            transcendentals=heads * rows * rows,
        ),
        name="project_and_own_block",
    )(events, events, w_in, rel_bias, lengths, asked)
    cand = jnp.dot(
        own_hits, arrived_rows.reshape(count * cap, width), preferred_element_type=f32
    ).astype(bf)
    layer_output, next_score, scores = pl.pallas_call(
        functools.partial(second_kernel, count),
        out_shape=(
            jax.ShapeDtypeStruct((rows, width), bf),
            jax.ShapeDtypeStruct((rows // TILE, 1, TILE), f32),
            jax.ShapeDtypeStruct((rows, candidates.shape[1]), f32),
        ),
        in_specs=[sm, sm, sm, vm, vm, vm, vm, vm, vm, hb, hb, hb],
        out_specs=(vm, vm, vm),
        scratch_shapes=[
            pltpu.VMEM((picks, rows, width), bf),
            pltpu.VMEM((width, 2 * width), bf),
            pltpu.VMEM((width, width), bf),
            pltpu.VMEM((rows, width), bf),
            pltpu.VMEM((rows, 2 * width), bf),
            pltpu.VMEM((rows, width), f32),
            pltpu.VMEM((heads, 2 * TILE, 6 * TILE), f32),
            pltpu.VMEM((rows, PAIR), bf),
            pltpu.VMEM((rows, PAIR), bf),
            pltpu.VMEM((rows, width), f32),
            pltpu.SemaphoreType.DMA((picks + 2,)),
        ],
        compiler_params=pltpu.CompilerParams(vmem_limit_bytes=VMEM_LIMIT),
        cost_estimate=pl.CostEstimate(
            flops=2 * picks * (2 * rows * width * width + 2 * rows * rows * width),
            bytes_accessed=16 * width * width,
            transcendentals=2 * heads * rows * rows,
        ),
        name="earlier_blocks_and_output",
    )(
        block_lists, lengths, rel_bias, events, gate, q, own, following, cand, w_in, w_out, recv,
    )
    return (layer_output, next_score.reshape(rows), scores)


def solution(mesh):
    in_specs = (
        P(("groups", "ctx"), None),
        P(),
        P(),
        P(),
        P("groups"),
        P(("groups", "ctx"), None),
        P("groups", None),
    )
    out_specs = (P(("groups", "ctx"), None), P(("groups", "ctx")), P(("groups", "ctx"), None))
    return jax.shard_map(shards, mesh=mesh, in_specs=in_specs, out_specs=out_specs, check_vma=False)
```

```python
import functools

import jax
import jax.numpy as jnp
from jax import lax
from jax.experimental import pallas as pl
from jax.experimental.pallas import tpu as pltpu
from jax.sharding import PartitionSpec as P

SPAN = 4
NEG = -1e30
TILE = 128
PAIR = 128
VMEM_LIMIT = 56 * 1024 * 1024
CHUNKS = 8
MESH = pl.DeviceIdType.MESH

NT = (((1,), (1,)), ((), ()))


def ends_of(lengths_ref):
    ends, total = [], 0
    for u in range(lengths_ref.shape[0]):
        total = total + lengths_ref[u]
        ends.append(total)
    return ends


def user_of(positions, ends):
    user = jnp.zeros_like(positions)
    for end in ends:
        user = user + (positions >= end).astype(jnp.int32)
    return user


def block_time(block, count):
    return lax.rem(block + count // 4, count)


def user_terms(time, rows, ends):
    row = lax.broadcasted_iota(jnp.int32, (rows, PAIR), 0)
    lane = lax.rem(lax.broadcasted_iota(jnp.int32, (rows, PAIR), 1), PAIR // 2)
    same = lane == user_of(time * rows + row, ends)
    one = jnp.where(same, 1.0, 0.0).astype(jnp.bfloat16)
    other = jnp.where(same, 0.0, NEG).astype(jnp.bfloat16)
    return other, one


def half_silu(u):
    return u * jnp.tanh(u) + u


def normalize(x):
    center = x - jnp.mean(x, -1, keepdims=True)
    spread = jnp.mean(center * center, -1, keepdims=True)
    return center * lax.rsqrt(spread + 1e-05)


def bucket_of(distance, buckets):
    return min(int(distance).bit_length(), buckets - 1) if distance > 0 else 0


def bias_tile(rel_ref, head, step, buckets):
    if step < 0:
        return jnp.full((TILE, TILE), NEG, jnp.float32)
    row = lax.broadcasted_iota(jnp.int32, (TILE, TILE), 0)
    col = lax.broadcasted_iota(jnp.int32, (TILE, TILE), 1)
    diff = row - col
    first = bucket_of(step * TILE - TILE + 1, buckets)
    last = bucket_of(step * TILE + TILE - 1, buckets)
    value = jnp.full((TILE, TILE), rel_ref[head, first] * 0.5, jnp.float32)
    for b in range(first + 1, last + 1):
        value = jnp.where(diff >= 2 ** (b - 1) - step * TILE, rel_ref[head, b] * 0.5, value)
    if step == 0:
        value = jnp.where(diff >= 0, value, NEG)
    return value


def fill_slab(slab, index, rel_ref, head, top, width, buckets):
    for step in range(top - width + 1, top + 2):
        tile = bias_tile(rel_ref, head, step, buckets)
        for a in range(2):
            p = top + a - step
            if 0 <= p < width:
                slab[index, a * TILE : (a + 1) * TILE, p * TILE : (p + 1) * TILE] = tile


def pair_operands(q, k, v, qm, hot):
    low = lax.broadcasted_iota(jnp.int32, (1, PAIR), 1) < PAIR // 2
    zero = jnp.zeros((), jnp.bfloat16)
    for side in range(2):
        mine = low if side == 0 else jnp.logical_not(low)
        yield (
            jnp.where(mine, q, qm),
            jnp.where(mine, k, hot),
            jnp.where(mine, v, zero),
        )


def first_kernel(
    count, x_ref, x_hbm, w_hbm, rel_ref, len_ref, picks_ref, gate_ref, q_ref, att_ref, recv, head_ref, cand_recv,
    w, normed, k_ref, v_ref, slab, qm_ref, hot_ref, fetched, sems, send_sem, recv_sem, head_sem, cand_send, cand_sem,
):
    rows, width = x_ref.shape
    heads, buckets = rel_ref.shape
    piece = rows // CHUNKS
    me = lax.axis_index("ctx")
    place, plane = lax.rem(me, SPAN), me // SPAN
    planes = count // SPAN
    shift = planes // 4

    def flows(of):
        later = lax.rem(of + shift, planes) + 1
        return jnp.logical_and(later < planes, later != planes // 2)

    sends = flows(plane)
    fed = flows(lax.rem(plane + planes - 1, planes))
    odd = lax.rem(place, 2)
    low = place < 2
    ahead = lax.rem(me + SPAN, count)
    before = lax.rem(me + count - 1, count)
    beside = me + 1 - 2 * odd
    opposite = jnp.where(low, me + 2, me - 2)
    relayed = jnp.logical_or(place >= 2, fed)

    barrier = pltpu.get_barrier_semaphore()

    def greet(j, carry):
        other = lax.rem(me + j, count)
        pl.semaphore_signal(barrier, inc=1, device_id={"ctx": other}, device_id_type=MESH)
        return carry

    lax.fori_loop(1, count, greet, 0)
    pl.semaphore_wait(barrier, count - 1)

    def part(c):
        return pl.ds(c * piece, piece)

    kinds = {
        0: (sends, None, 3, ahead),
        1: (low, None, 1, opposite),
        2: (odd == 0, None, 0, beside),
        3: (jnp.logical_and(place >= 2, fed), 3, 1, opposite),
        4: (jnp.logical_and(odd == 1, fed), 3, 2, beside),
        5: (jnp.logical_and(relayed, odd == 0), 1, 2, beside),
        6: (jnp.logical_and(relayed, odd == 1), 1, 0, beside),
    }

    def sending(kind, c):
        _, source, slot, to = kinds[kind]
        return pltpu.make_async_remote_copy(
            src_ref=x_hbm.at[part(c)] if source is None else recv.at[source, part(c)],
            dst_ref=recv.at[slot, part(c)],
            send_sem=send_sem.at[kind, c],
            recv_sem=recv_sem.at[slot, c],
            device_id={"ctx": to},
            device_id_type=MESH,
        )

    def start(kind, c):
        @pl.when(kinds[kind][0])
        def _():
            sending(kind, c).start()

    def arrived(slot, c, when):
        @pl.when(when)
        def _():
            pltpu.make_async_copy(
                recv.at[slot, part(c)], recv.at[slot, part(c)], recv_sem.at[slot, c]
            ).wait()

    def earlier(c):
        arrived(3, c, fed)
        start(3, c)
        start(4, c)

    def relay(c):
        arrived(1, c, relayed)
        start(5, c)
        start(6, c)

    for c in range(CHUNKS):
        start(0, c)
        start(1, c)
    for c in range(CHUNKS):
        start(2, c)
    heading = pltpu.make_async_remote_copy(
        src_ref=x_hbm.at[pl.ds(0, 16)],
        dst_ref=head_ref,
        send_sem=head_sem.at[0],
        recv_sem=head_sem.at[1],
        device_id={"ctx": before},
        device_id_type=MESH,
    )
    heading.start()
    cap = picks_ref.shape[0] // count
    fetched[...] = (
        jnp.dot(picks_ref[...], x_ref[...], preferred_element_type=jnp.float32)
        .astype(jnp.bfloat16)
        .reshape(count, cap, width)
    )

    def candidate(j):
        to = lax.rem(me + j, count)
        return pltpu.make_async_remote_copy(
            src_ref=fetched.at[to],
            dst_ref=cand_recv.at[me],
            send_sem=cand_send.at[j],
            recv_sem=cand_sem.at[me],
            device_id={"ctx": to},
            device_id_type=MESH,
        )

    def send_candidate(j, carry):
        candidate(j).start()
        return carry

    lax.fori_loop(1, count, send_candidate, 0)
    own_rows = pltpu.make_async_copy(fetched.at[me], cand_recv.at[me], cand_send.at[0])
    own_rows.start()
    order = (1, 3, 2, 0)
    copies = {
        g: pltpu.make_async_copy(
            w_hbm.at[:, g * width : (g + 1) * width], w.at[g], sems.at[g]
        )
        for g in order
    }
    for g in order:
        copies[g].start()
    normed[...] = normalize(x_ref[...].astype(jnp.float32)).astype(jnp.bfloat16)
    qm_ref[...], hot_ref[...] = user_terms(block_time(me, count), rows, ends_of(len_ref))

    def project(g, out, scale):
        def step(j, carry):
            cols = pl.ds(pl.multiple_of(j * 256, 256), 256)
            u = 0.5 * jnp.dot(normed[...], w[g, :, cols], preferred_element_type=jnp.float32)
            y = half_silu(u).astype(jnp.bfloat16)
            out[:, cols] = y if scale is None else y * jnp.asarray(scale, jnp.bfloat16)
            return carry

        copies[g].wait()
        lax.fori_loop(0, width // 256, step, 0)

    project(1, q_ref, 0.5 * (width // heads) ** -0.5)
    project(3, k_ref, None)
    project(2, v_ref, None)
    earlier(0)
    project(0, gate_ref, None)
    earlier(1)

    half = rows // 2

    def pair(hp, carry):
        cols = pl.ds(pl.multiple_of(hp * PAIR, PAIR), PAIR)
        for side in range(2):
            fill_slab(slab, side, rel_ref, 2 * hp + side, 2, 4, buckets)
        tops = []
        for side, (q, k, v) in enumerate(
            pair_operands(q_ref[:, cols], k_ref[:, cols], v_ref[:, cols], qm_ref[...], hot_ref[...])
        ):
            s0 = lax.dot_general(q[:half], k[:half], NT, preferred_element_type=jnp.float32)
            s1 = lax.dot_general(q[half:], k, NT, preferred_element_type=jnp.float32)
            w0 = half_silu(s0 + slab[side, :, half:]).astype(jnp.bfloat16)
            w1 = half_silu(s1 + slab[side]).astype(jnp.bfloat16)
            tops.append(
                (
                    jnp.dot(w0, v[:half], preferred_element_type=jnp.float32),
                    jnp.dot(w1, v, preferred_element_type=jnp.float32),
                )
            )
        att_ref[:half, cols] = tops[0][0] + tops[1][0]
        att_ref[half:, cols] = tops[0][1] + tops[1][1]
        return carry

    pairs = heads // 2
    lax.fori_loop(0, pairs // 4, pair, 0)
    earlier(2)
    relay(0)
    lax.fori_loop(pairs // 4, pairs * 5 // 8, pair, 0)
    earlier(3)
    relay(1)
    lax.fori_loop(pairs * 5 // 8, pairs, pair, 0)
    for c in range(4, CHUNKS):
        earlier(c)
        relay(c - 2)
    relay(CHUNKS - 2)
    relay(CHUNKS - 1)

    def end_candidate(j, carry):
        source = lax.rem(me + j, count)
        pltpu.make_async_copy(
            cand_recv.at[source], cand_recv.at[source], cand_sem.at[source]
        ).wait()
        candidate(j).wait_send()
        return carry

    own_rows.wait()
    lax.fori_loop(1, count, end_candidate, 0)
    for c in range(CHUNKS):
        arrived(0, c, jnp.logical_or(odd == 1, relayed))
        arrived(2, c, jnp.logical_or(place == 3, fed))
        for kind in kinds:
            @pl.when(kinds[kind][0])
            def _(kind=kind, c=c):
                sending(kind, c).wait_send()
    heading.wait()


def second_kernel(
    count, list_ref, len_ref, rel_ref, x_ref, gate_ref, q_ref, own_ref, head_ref, cand_ref,
    w_hbm, wout_hbm, recv, out_ref, next_ref, table_ref,
    picked, wkv, wout, normed, kv, att, slab, qm_ref, hot_ref, follow, sems,
):
    rows, width = x_ref.shape
    heads, buckets = rel_ref.shape
    picks = list_ref.shape[1]
    half = rows // 2
    ends = ends_of(len_ref)
    time = block_time(lax.axis_index("ctx"), count)
    useful = []
    for p in range(picks):
        distance = list_ref[0, p]
        last = (time - distance + 1) * rows - 1
        useful.append((distance <= time) & (user_of(last, ends) >= user_of(time * rows, ends)))

        @pl.when(useful[p])
        def _(p=p, distance=distance):
            pltpu.make_async_copy(recv.at[distance - 1], picked.at[p], sems.at[p]).start()
    w_copy = pltpu.make_async_copy(w_hbm.at[:, 2 * width :], wkv, sems.at[picks])
    o_copy = pltpu.make_async_copy(wout_hbm, wout, sems.at[picks + 1])
    w_copy.start()
    o_copy.start()
    att[...] = own_ref[...]
    qm_ref[...] = user_terms(time, rows, ends)[0]
    w_copy.wait()
    for p in range(picks):
        @pl.when(useful[p])
        def _(p=p):
            distance = list_ref[0, p]
            pltpu.make_async_copy(recv.at[0], picked.at[p], sems.at[p]).wait()
            hot_ref[...] = user_terms(time - distance, rows, ends)[1]
            normed[...] = normalize(picked[p].astype(jnp.float32)).astype(jnp.bfloat16)

            def step(j, carry):
                cols = pl.ds(pl.multiple_of(j * 256, 256), 256)
                u = 0.5 * jnp.dot(normed[...], wkv[:, cols], preferred_element_type=jnp.float32)
                kv[:, cols] = half_silu(u).astype(jnp.bfloat16)
                return carry

            lax.fori_loop(0, 2 * width // 256, step, 0, unroll=2)
            for d in range(1, SPAN + 1):
                @pl.when(distance == d)
                def _(d=d):
                    def fill(h, carry):
                        fill_slab(slab, h, rel_ref, h, (rows // TILE) * d + 2, 6, buckets)
                        return carry

                    lax.fori_loop(0, heads, fill, 0)

            def pair(hp, carry):
                cols = pl.ds(pl.multiple_of(hp * PAIR, PAIR), PAIR)
                kcols = pl.ds(pl.multiple_of(width + hp * PAIR, PAIR), PAIR)
                tops = []
                for side, (q, k, v) in enumerate(
                    pair_operands(q_ref[:, cols], kv[:, kcols], kv[:, cols], qm_ref[...], hot_ref[...])
                ):
                    h = 2 * hp + side
                    s0 = lax.dot_general(q[:half], k, NT, preferred_element_type=jnp.float32)
                    s1 = lax.dot_general(q[half:], k, NT, preferred_element_type=jnp.float32)
                    w0 = half_silu(s0 + slab[h, :, half:]).astype(jnp.bfloat16)
                    w1 = half_silu(s1 + slab[h, :, :rows]).astype(jnp.bfloat16)
                    tops.append(
                        (
                            jnp.dot(w0, v, preferred_element_type=jnp.float32),
                            jnp.dot(w1, v, preferred_element_type=jnp.float32),
                        )
                    )
                att[:half, cols] += tops[0][0] + tops[1][0]
                att[half:, cols] += tops[0][1] + tops[1][1]
                return carry

            lax.fori_loop(0, heads // 2, pair, 0, unroll=2)
    o_copy.wait()
    scale = width**-0.5
    last_row = lax.broadcasted_iota(jnp.int32, (rows, 1), 0) == rows - 1
    follow[...] = jnp.where(
        last_row,
        head_ref[0:1, :].astype(jnp.float32),
        pltpu.roll(x_ref[...].astype(jnp.float32), rows - 1, 0),
    )

    def finish(r, carry):
        rs = pl.ds(pl.multiple_of(r * 256, 256), 256)
        gated = (normalize(att[rs, :]) * gate_ref[rs, :].astype(jnp.float32)).astype(jnp.bfloat16)
        added = jnp.dot(gated, wout[...], preferred_element_type=jnp.float32)
        layer = (x_ref[rs, :].astype(jnp.float32) + added).astype(jnp.bfloat16)
        out_ref[rs, :] = layer
        inner = jnp.sum(
            layer.astype(jnp.float32) * follow[rs, :], axis=1, keepdims=True
        )
        at = time * rows + r * 256 + lax.broadcasted_iota(jnp.int32, (256, 1), 0)
        same = (user_of(at + 1, ends) == user_of(at, ends)) & (at + 1 < count * rows)
        score = jnp.where(same, inner * scale, 0.0)
        eye = lax.broadcasted_iota(jnp.int32, (TILE, TILE), 0) == lax.broadcasted_iota(
            jnp.int32, (TILE, TILE), 1
        )
        for j in range(256 // TILE):
            spread = jnp.where(eye, score[j * TILE : (j + 1) * TILE], 0.0)
            next_ref[r * (256 // TILE) + j] = jnp.sum(spread, axis=0, keepdims=True)
        table_ref[rs, :] = (
            lax.dot_general(layer, cand_ref[...], NT, preferred_element_type=jnp.float32) * scale
        )
        return carry

    lax.fori_loop(0, rows // 256, finish, 0, unroll=2)


def candidate_slots(candidates, event_row_count, ctx_size, my_index):
    cand_count = candidates.shape[1]
    slot_cap = max(2 * cand_count // ctx_size, 16)
    number = jnp.arange(cand_count, dtype=jnp.int32)
    before = number[:, None] < number[None, :]
    mine = candidates // event_row_count == my_index
    rank = jnp.dot(
        mine.astype(jnp.bfloat16), before.astype(jnp.bfloat16), preferred_element_type=jnp.float32
    ).astype(jnp.int32)
    local = jnp.where(mine, candidates % event_row_count, -1)
    slots = jnp.arange(slot_cap, dtype=jnp.int32)
    ids = jnp.max(
        jnp.where(rank[:, None, :] == slots[None, :, None], local[:, None, :], -1), axis=2
    ).reshape(-1)
    picks = (ids[:, None] == jnp.arange(event_row_count, dtype=jnp.int32)[None, :]).astype(jnp.bfloat16)
    owner = lax.dynamic_slice_in_dim(candidates, my_index, 1, 0)[0] // event_row_count
    own_rank = jnp.sum(
        ((owner[:, None] == owner[None, :]) & before.T).astype(jnp.int32), axis=1
    )
    own_slot = owner * slot_cap + own_rank
    own_hits = own_slot[:, None] == jnp.arange(ctx_size * slot_cap, dtype=jnp.int32)[None, :]
    return picks, own_hits.astype(jnp.bfloat16)


def shards(events, w_in, w_out, rel_bias, lengths, block_lists, candidates):
    rows, width = events.shape
    heads = rel_bias.shape[0]
    picks = block_lists.shape[1]
    count = lax.axis_size("ctx")
    asked, own_hits = candidate_slots(candidates, rows, count, lax.axis_index("ctx"))
    cap = asked.shape[0] // count

    vm = pl.BlockSpec(memory_space=pltpu.VMEM)
    sm = pl.BlockSpec(memory_space=pltpu.SMEM)
    hb = pl.BlockSpec(memory_space=pl.ANY)
    bf, f32 = jnp.bfloat16, jnp.float32
    gate, q, own, recv, following, arrived_rows = pl.pallas_call(
        functools.partial(first_kernel, count),
        out_shape=(
            jax.ShapeDtypeStruct((rows, width), bf),
            jax.ShapeDtypeStruct((rows, width), bf),
            jax.ShapeDtypeStruct((rows, width), f32),
            jax.ShapeDtypeStruct((SPAN, rows, width), bf),
            jax.ShapeDtypeStruct((16, width), bf),
            jax.ShapeDtypeStruct((count, cap, width), bf),
        ),
        in_specs=[vm, hb, hb, sm, sm, vm],
        out_specs=(vm, vm, vm, hb, hb, hb),
        scratch_shapes=[
            pltpu.VMEM((4, width, width), bf),
            pltpu.VMEM((rows, width), bf),
            pltpu.VMEM((rows, width), bf),
            pltpu.VMEM((rows, width), bf),
            pltpu.VMEM((2, 2 * TILE, 4 * TILE), f32),
            pltpu.VMEM((rows, PAIR), bf),
            pltpu.VMEM((rows, PAIR), bf),
            pltpu.VMEM((count, cap, width), bf),
            pltpu.SemaphoreType.DMA((4,)),
            pltpu.SemaphoreType.DMA((7, CHUNKS)),
            pltpu.SemaphoreType.DMA((SPAN, CHUNKS)),
            pltpu.SemaphoreType.DMA((2,)),
            pltpu.SemaphoreType.DMA((count,)),
            pltpu.SemaphoreType.DMA((count,)),
        ],
        compiler_params=pltpu.CompilerParams(
            vmem_limit_bytes=VMEM_LIMIT, collective_id=0, has_side_effects=True
        ),
        cost_estimate=pl.CostEstimate(
            flops=2 * rows * width * 4 * width + 4 * rows * rows * width,
            bytes_accessed=10 * width * width,
            transcendentals=heads * rows * rows,
        ),
        name="project_and_own_block",
    )(events, events, w_in, rel_bias, lengths, asked)
    cand = jnp.dot(
        own_hits, arrived_rows.reshape(count * cap, width), preferred_element_type=f32
    ).astype(bf)
    layer_output, next_score, scores = pl.pallas_call(
        functools.partial(second_kernel, count),
        out_shape=(
            jax.ShapeDtypeStruct((rows, width), bf),
            jax.ShapeDtypeStruct((rows // TILE, 1, TILE), f32),
            jax.ShapeDtypeStruct((rows, candidates.shape[1]), f32),
        ),
        in_specs=[sm, sm, sm, vm, vm, vm, vm, vm, vm, hb, hb, hb],
        out_specs=(vm, vm, vm),
        scratch_shapes=[
            pltpu.VMEM((picks, rows, width), bf),
            pltpu.VMEM((width, 2 * width), bf),
            pltpu.VMEM((width, width), bf),
            pltpu.VMEM((rows, width), bf),
            pltpu.VMEM((rows, 2 * width), bf),
            pltpu.VMEM((rows, width), f32),
            pltpu.VMEM((heads, 2 * TILE, 6 * TILE), f32),
            pltpu.VMEM((rows, PAIR), bf),
            pltpu.VMEM((rows, PAIR), bf),
            pltpu.VMEM((rows, width), f32),
            pltpu.SemaphoreType.DMA((picks + 2,)),
        ],
        compiler_params=pltpu.CompilerParams(vmem_limit_bytes=VMEM_LIMIT),
        cost_estimate=pl.CostEstimate(
            flops=2 * picks * (2 * rows * width * width + 2 * rows * rows * width),
            bytes_accessed=16 * width * width,
            transcendentals=2 * heads * rows * rows,
        ),
        name="earlier_blocks_and_output",
    )(
        block_lists, lengths, rel_bias, events, gate, q, own, following, cand, w_in, w_out, recv,
    )
    return (layer_output, next_score.reshape(rows), scores)


def solution(mesh):
    in_specs = (
        P(("groups", "ctx"), None),
        P(),
        P(),
        P(),
        P("groups"),
        P(("groups", "ctx"), None),
        P("groups", None),
    )
    out_specs = (P(("groups", "ctx"), None), P(("groups", "ctx")), P(("groups", "ctx"), None))
    return jax.shard_map(shards, mesh=mesh, in_specs=in_specs, out_specs=out_specs, check_vma=False)
```
